32 devices in a mesh: col: 16 (over z, x, core), row: 2 (over y).
Axes of the slice: x: 2, y: 2, z: 4, core: 2. Of those that a mesh axis runs over, the one named last changes fastest.
Arguments:
- covering_tiles: bfloat16 [2, 1024, 128, 128], P('row', 'col'), may hold values from -0.09375 to 0.09375
- tile_row_blocks: int32 [2, 1024], P('row', 'col'), may hold values from 0 to 31
- tile_cols: int32 [2, 1024], P('row', 'col'), may hold values from 0 to 63
- cut_tiles: bfloat16 [16, 128, 128, 128], P('col', 'row'), may hold values from -0.0625 to 0.0625
- cut_dest: int32 [16, 128, 1], P('col', 'row'), may hold values from 0 to 15; in each aligned block of 64 rows (0 to 63, 64 to 127, ..., all dimensions but the last counted through in order) at most 8 rows name the same one
- cut_cols: int32 [16, 128], P('col', 'row'), may hold values from 0 to 63
- cost: float32 [1024, 128], P('col'), may hold values from -30 to 30
- demand: float32 [64, 128], P('row'), may hold values from 0 to 12
- primal_start: float32 [1024, 128], P('col'), may hold values from 0 to 1
- initial_duals: float32 [64, 128], P('row'), may hold values from 0 to 1
- cut_start: float32 [16, 256], P('col', 'row'), may hold values from 0 to 1
- primal_weight: float32 [1], replicated, may hold values from 0.5 to 2
- step_size: float32 [1], replicated, may hold values from 0.3 to 0.6
- exponents: int32 [1024], P('col'), may hold values from 0 to 3
Outputs:
- primal: float32 [1024, 128], P('col')
- dual: float32 [64, 128], P('row')
- cut_dual: float32 [16, 256], P('col', 'row')
- violation: float32 [1024, 128], P('col')
The draws below stay inside these ranges and needn't reach their ends.
Inputs may be any that keep to these rules, and one draw needn't show every extreme that they name: `cut_dest`: the cut tiles of one device touch at most 8 times the same column shard; some device reaches 8.
All inputs are finite; a program needn't handle non-finite values.
Results may differ from the reference program's by a relative error of at most 0.0017.
The reference program's roundings to bfloat16 on the way (of `xbar`) count: a program that leaves them out, or rounds other values in their place, can miss the bound.
Values may be sent and summed in bfloat16 or wider, within the bound.
A program may use at most 64 MiB of HBM per device.

```python
import math
import jax
import jax.numpy as jnp
import numpy as np
from jax import lax

TILE_SIDE = 128
NCB = 64
ROW_BLOCK_LIMIT = 32
TILES_PER_SHARD = 64
CUT_DEV = 64
ITERS = 2
CAP = 8
N_COL = 16
N_ROW = 2


def draw_cost(key, part):
    key = jax.random.fold_in(key, 11)
    first, second = jax.random.split(key)
    tally_number = N_COL * NCB * TILE_SIDE
    frac = jnp.arange(tally_number, dtype=jnp.float32) / (tally_number - 1)
    spread_values = jnp.exp(jax.random.uniform(first, (tally_number,), jnp.float32) * math.log(10.0))
    offset_start = jax.random.normal(second, (tally_number,), jnp.float32)
    increase_amount = 1.0 + 2.0 * frac
    return (0.15 * spread_values * increase_amount * offset_start).reshape(N_COL * NCB, TILE_SIDE)


def draw_demand(key, part):
    key = jax.random.fold_in(key, 23)
    first, second = jax.random.split(key)
    tally_number = N_ROW * ROW_BLOCK_LIMIT * TILE_SIDE
    frac = jnp.arange(tally_number, dtype=jnp.float32) / (tally_number - 1)
    spread_values = jnp.exp(jax.random.uniform(first, (tally_number,), jnp.float32) * math.log(10.0))
    offset_start = 0.5 + jax.random.uniform(second, (tally_number,), jnp.float32)
    increase_amount = 1.0 + 2.0 * frac
    return (0.15 * spread_values * increase_amount * offset_start).reshape(N_ROW * ROW_BLOCK_LIMIT, TILE_SIDE)


def set_ends(values, rng, smallest, top_value):
    dims = values.shape
    index_at = [jax.random.randint(jax.random.fold_in(rng, axis), (), 0, dims[axis]) for axis in range(len(dims))]
    values = values.at[tuple(index_at)].set(smallest)
    longest = dims.index(max(dims))
    index_at[longest] = (index_at[longest] + 1) % dims[longest]
    return values.at[tuple(index_at)].set(top_value)


def steps_of(stream_key, shape, cuts, least, high):
    loudness = 1.0
    for dim, shards_of in cuts:
        draws = jax.random.uniform(jax.random.fold_in(jax.random.fold_in(stream_key, 6), dim), (shards_of,), jnp.float32, least / len(cuts), high / len(cuts))
        loudness = loudness * jnp.repeat(jnp.exp(draws), shape[dim] // shards_of).reshape((-1,) + (1,) * (len(shape) - 1 - dim))
    return loudness


def shared_out(key, own, number, rows, amount, top, most, skew):
    sequence = jax.random.permutation(key, amount)
    packed, usual = shares(amount, rows * top, most, skew, True), shares(amount, rows * top, most, skew, False)
    places = jnp.arange(amount)

    def named(sizes, rotation):
        used = int((sizes > 0).sum())
        fixed = max(1, used // 4)
        moved = fixed + (places - fixed + rotation * (used - fixed)) % max(1, amount - fixed)
        return jnp.zeros((amount,), jnp.int32).at[sequence[jnp.where(places < fixed, places, moved)]].set(jnp.asarray(sizes, jnp.int32))

    sizes = jnp.where(number % 4 == 0, named(packed, number // 4), named(usual, number - number // 4 - 1))
    mixed = jax.random.permutation(jax.random.fold_in(own, 3), amount)
    giver, receiver = mixed[0:amount // 2 * 2:2], mixed[1:amount // 2 * 2:2]
    margin = jnp.minimum(sizes[giver] - 1, most - sizes[receiver]) // 2
    margin = jnp.where((giver == sequence[0]) | (receiver == sequence[0]) | (sizes[receiver] == 0), 0, jnp.maximum(margin, 0))
    moved = jax.random.randint(jax.random.fold_in(own, 4), (amount // 2,), 0, 1 << 20) % (margin + 1)
    sizes = sizes.at[giver].add(-moved).at[receiver].add(moved)
    items = jnp.searchsorted(jnp.cumsum(sizes), jnp.arange(rows * top), side="right").astype(jnp.int32)
    listing = items.reshape(top, rows).T
    listing = listing[jax.random.permutation(jax.random.fold_in(own, 1), rows)]
    rotation = jax.random.randint(jax.random.fold_in(own, 2), (rows, 1), 0, top)
    return jnp.take_along_axis(listing, (jnp.arange(top)[None, :] + rotation) % top, axis=1)


def shares(number_of, total, reach, lean, full):
    loads = [(1 << 20) // math.isqrt(standing ** lean) + 1 for standing in range(1, number_of + 1)]
    largest = reach if full else min(reach, max(-(-total // number_of), total * loads[0] // sum(loads)))
    least = 1 if total - largest >= number_of - 1 else 0
    holding, surplus = [largest] + [least] * (number_of - 1), total - largest - least * (number_of - 1)
    while surplus > 0:
        candidates = [i for i in range(1, number_of) if holding[i] < largest] or [i for i in range(1, number_of) if holding[i] < reach]
        pool, remaining = sum([loads[i] for i in candidates]), surplus
        for i in candidates:
            extra = min(reach - holding[i], max(1, remaining * loads[i] // pool), surplus)
            holding[i] = holding[i] + extra
            surplus = surplus - extra
    return np.array(holding)


def scatter_about(own_key, extent, scale, bound, cuts=(), held_as=jnp.bfloat16):
    drawn = jax.random.normal(own_key, extent, jnp.float32) * scale
    if len(cuts) > 0:
        drawn = steps_of(own_key, extent, cuts, -0.22, 0.18) * drawn
    return jnp.clip(drawn, min=-bound, max=bound).astype(held_as)


def setup_inputs(seed: int = 0) -> dict:
    splits = jax.random.split(jax.random.key(seed), 15)
    covering_tiles = scatter_about(splits[0], (N_ROW, N_COL * TILES_PER_SHARD, TILE_SIDE, TILE_SIDE), (TILES_PER_SHARD * N_COL * TILE_SIDE // ROW_BLOCK_LIMIT) ** -0.5, 0.09375, ((0, 2), (1, 16)))
    tile_row_blocks = set_ends(jax.random.randint(splits[1], (N_ROW, N_COL * TILES_PER_SHARD), 0, ROW_BLOCK_LIMIT), jax.random.fold_in(splits[1], 1), 0, ROW_BLOCK_LIMIT - 1).astype(jnp.int32)
    tile_cols = set_ends(jax.random.randint(splits[2], (N_ROW, N_COL * TILES_PER_SHARD), 0, NCB), jax.random.fold_in(splits[2], 1), 0, NCB - 1).astype(jnp.int32)
    cut_tiles = scatter_about(splits[3], (N_COL, N_ROW * CUT_DEV, TILE_SIDE, TILE_SIDE), (CUT_DEV * TILE_SIDE) ** -0.5, 0.0625, ((0, 16), (1, 2)))
    cut_dest_keys = jax.random.split(jax.random.fold_in(splits[4], 1), N_COL * (N_ROW * CUT_DEV) // CUT_DEV)
    cut_dest_turns = jax.random.permutation(jax.random.fold_in(splits[4], 3), N_COL * (N_ROW * CUT_DEV) // CUT_DEV)
    cut_dest = jax.vmap(lambda own, number: shared_out(jax.random.fold_in(splits[4], 2), own, number, CUT_DEV, N_COL, 1, CAP, 0))(cut_dest_keys, cut_dest_turns).reshape((N_COL, N_ROW * CUT_DEV, 1))
    cut_cols = set_ends(jax.random.randint(splits[5], (N_COL, N_ROW * CUT_DEV), 0, NCB), jax.random.fold_in(splits[5], 1), 0, NCB - 1).astype(jnp.int32)
    cost = draw_cost(jax.random.fold_in(splits[14], 71), 0)
    demand = draw_demand(jax.random.fold_in(splits[14], 71), 0)
    primal_start = jnp.clip(1.0 * jax.random.uniform(splits[8], (N_COL * NCB, TILE_SIDE), jnp.float32) ** steps_of(splits[8], (N_COL * NCB, TILE_SIDE), ((0, 16),), -0.2, 0.2), 0.0, 1.0)
    initial_duals = jnp.clip(1.0 * jax.random.uniform(splits[9], (N_ROW * ROW_BLOCK_LIMIT, TILE_SIDE), jnp.float32) ** steps_of(splits[9], (N_ROW * ROW_BLOCK_LIMIT, TILE_SIDE), ((0, 2),), -0.2, 0.2), 0.0, 1.0)
    cut_start = jnp.clip(1.0 * jax.random.uniform(splits[10], (N_COL, N_ROW * TILE_SIDE), jnp.float32) ** steps_of(splits[10], (N_COL, N_ROW * TILE_SIDE), ((0, 16), (1, 2)), -0.2, 0.2), 0.0, 1.0)
    primal_weight = jnp.clip(jnp.exp(jax.random.uniform(splits[11], (1,), jnp.float32, math.log(0.5), math.log(2.0))), 0.5, 2.0)
    step_size = jnp.clip(jax.random.uniform(splits[12], (1,), jnp.float32, 0.3, 0.6), 0.3, 0.6)
    exponents = set_ends(jax.random.randint(splits[13], (N_COL * NCB,), 0, 4), jax.random.fold_in(splits[13], 1), 0, 3).astype(jnp.int32)
    return dict(covering_tiles=covering_tiles, tile_row_blocks=tile_row_blocks, tile_cols=tile_cols, cut_tiles=cut_tiles, cut_dest=cut_dest, cut_cols=cut_cols, cost=cost, demand=demand, primal_start=primal_start, initial_duals=initial_duals, cut_start=cut_start, primal_weight=primal_weight, step_size=step_size, exponents=exponents)


def row_terms(covering_tiles, tile_row_blocks, tile_cols, xbar):
    owner = jnp.arange(N_COL * TILES_PER_SHARD, dtype=jnp.int32) // TILES_PER_SHARD

    def unit_value(row_position):
        tiles = covering_tiles[row_position].astype(jnp.float32)
        gcols = (owner * NCB + tile_cols[row_position]).astype(jnp.int32)
        entry_values = jnp.einsum('tij,tj->ti', tiles, xbar[gcols].astype(jnp.float32))
        return jax.ops.segment_sum(entry_values, tile_row_blocks[row_position], num_segments=ROW_BLOCK_LIMIT)
    return lax.map(unit_value, jnp.arange(N_ROW, dtype=jnp.int32)).reshape(N_ROW * ROW_BLOCK_LIMIT, TILE_SIDE)

def column_terms(covering_tiles, tile_row_blocks, tile_cols, ybar):
    owner = jnp.arange(N_COL * TILES_PER_SHARD, dtype=jnp.int32) // TILES_PER_SHARD

    def unit_value(carry, row_position):
        tiles = covering_tiles[row_position].astype(jnp.float32)
        growth_rows = (row_position * ROW_BLOCK_LIMIT + tile_row_blocks[row_position]).astype(jnp.int32)
        gcols = (owner * NCB + tile_cols[row_position]).astype(jnp.int32)
        entry_values = jnp.einsum('tij,ti->tj', tiles, ybar[growth_rows].astype(jnp.float32))
        return (carry + jax.ops.segment_sum(entry_values, gcols, num_segments=N_COL * NCB), None)
    start = jnp.zeros((N_COL * NCB, TILE_SIDE), jnp.float32)
    total, _ = lax.scan(unit_value, start, jnp.arange(N_ROW, dtype=jnp.int32))
    return total

def cut_columns(cut_tiles, cut_dest, cut_cols, wbar):
    which = jnp.arange(N_ROW * CUT_DEV, dtype=jnp.int32) // CUT_DEV

    def unit_value(carry, c):
        tiles = cut_tiles[c].astype(jnp.float32)
        wrows = wbar[c].reshape(N_ROW, TILE_SIDE)[which].astype(jnp.float32)
        entry_values = jnp.einsum('kij,ki->kj', tiles, wrows)
        gcols = (cut_dest[c, :, 0] * NCB + cut_cols[c]).astype(jnp.int32)
        return (carry + jax.ops.segment_sum(entry_values, gcols, num_segments=N_COL * NCB), None)
    start = jnp.zeros((N_COL * NCB, TILE_SIDE), jnp.float32)
    total, _ = lax.scan(unit_value, start, jnp.arange(N_COL, dtype=jnp.int32))
    return total

def cut_rows(cut_tiles, cut_dest, cut_cols, xbar):

    def unit_value(c):
        tiles = cut_tiles[c].astype(jnp.float32)
        gcols = (cut_dest[c, :, 0] * NCB + cut_cols[c]).astype(jnp.int32)
        entry_values = jnp.einsum('kij,kj->ki', tiles, xbar[gcols].astype(jnp.float32))
        return entry_values.reshape(N_ROW, CUT_DEV, TILE_SIDE).sum(axis=1).reshape(N_ROW * TILE_SIDE)
    return lax.map(unit_value, jnp.arange(N_COL, dtype=jnp.int32))

def reference(covering_tiles, tile_row_blocks, tile_cols, cut_tiles, cut_dest, cut_cols, cost, demand, primal_start, initial_duals, cut_start, primal_weight, step_size, exponents):
    primal = primal_start
    dual = initial_duals
    cut_dual = cut_start
    eta = step_size[0]
    omega = primal_weight[0]
    for turn in range(ITERS):
        ybar = dual.astype(jnp.bfloat16)
        wbar = cut_dual.astype(jnp.bfloat16)
        grad = cost - column_terms(covering_tiles, tile_row_blocks, tile_cols, ybar) + cut_columns(cut_tiles, cut_dest, cut_cols, wbar)
        tau = eta / omega
        sigma = eta * omega
        new_primal = jnp.clip(primal - tau * grad, 0.0, 1.0)
        xbar = (2.0 * new_primal - primal).astype(jnp.bfloat16)
        new_dual = jnp.maximum(dual + sigma * (demand - row_terms(covering_tiles, tile_row_blocks, tile_cols, xbar)), 0.0)
        new_cut = jnp.maximum(cut_dual + sigma * (cut_rows(cut_tiles, cut_dest, cut_cols, xbar) - 1.0), 0.0)
        if turn + 1 < ITERS:
            step_x = new_primal - primal
            step_y = new_dual - dual
            step_w = new_cut - cut_dual
            moved = jnp.sum(step_x * step_x)
            dual_moved = jnp.sum(step_y * step_y) + jnp.sum(step_w * step_w)
            omega = jnp.sqrt(omega * jnp.sqrt((moved + 1e-06) / (dual_moved + 1e-06)))
        primal, dual, cut_dual = (new_primal, new_dual, new_cut)
    ybar = dual.astype(jnp.bfloat16)
    wbar = cut_dual.astype(jnp.bfloat16)
    grad = cost - column_terms(covering_tiles, tile_row_blocks, tile_cols, ybar) + cut_columns(cut_tiles, cut_dest, cut_cols, wbar)
    limit = (-0.125 * jnp.exp2(exponents.astype(jnp.float32))).reshape(N_COL * NCB, 1)
    violation = jnp.maximum(limit - grad, 0.0)
    return (primal, dual, cut_dual, violation)
```

```python
import functools

import jax
import jax.numpy as jnp
from jax import lax
from jax.experimental import pallas as pl
from jax.experimental.pallas import tpu as pltpu
from jax.sharding import PartitionSpec as P

ITERS = 2
EPSILON = 1e-06
GROUP = 16
STRIDE = 8
BF = jnp.bfloat16
F32 = jnp.float32
MESH = pl.DeviceIdType.MESH


def dot(a, b, contract):
    return lax.dot_general(a, b, ((contract[:1], contract[1:]), ((), ())), preferred_element_type=F32)


def split3(values):
    high = values.astype(BF)
    rest = values - high.astype(F32)
    middle = rest.astype(BF)
    low = (rest - middle.astype(F32)).astype(BF)
    return high, middle, low


def spread(table, values, contract):
    high, middle, low = split3(values)
    return dot(table, high, contract) + (dot(table, middle, contract) + dot(table, low, contract))


def kernel(
    owners,
    n_row,
    tiles,
    row_of,
    col_of,
    cuts,
    dest,
    cut_col,
    cost,
    demand,
    x0,
    y0,
    w0,
    weight,
    step,
    exps,
    x_out,
    y_out,
    w_out,
    v_out,
    send_a,
    recv_a,
    send_x,
    recv_x,
    send_p,
    recv_p,
    send_r,
    recv_r,
    sem_a,
    sem_x,
    sem_p,
    sem_r,
):
    c = lax.axis_index("col")
    r = lax.axis_index("row")
    n_dev = owners * n_row
    flat = r * owners + c
    count = tiles.shape[1]
    blocks, width = cost.shape
    row_blocks = demand.shape[0]
    slots = owners * STRIDE

    barrier = pltpu.get_barrier_semaphore()

    def greet(k, carry):
        other = lax.rem(flat + k, n_dev)
        pl.semaphore_signal(
            barrier,
            inc=1,
            device_id={"col": lax.rem(other, owners), "row": other // owners},
            device_id_type=MESH,
        )
        return carry

    lax.fori_loop(1, n_dev, greet, 0)

    def one_hot(row, size):
        return jnp.where(
            lax.broadcasted_iota(jnp.int32, (size, row.shape[1]), 0) == row, 1.0, 0.0
        )

    row_table = one_hot(row_of[...], row_blocks).astype(BF)
    col_table = one_hot(col_of[...], blocks).astype(BF)
    owner_table = one_hot(dest[...], max(owners, 16)).astype(BF)
    same = dot(owner_table, owner_table, (0, 0))
    earlier = lax.broadcasted_iota(jnp.int32, same.shape, 0) < lax.broadcasted_iota(
        jnp.int32, same.shape, 1
    )
    rank = jnp.sum(jnp.where(earlier, same, 0.0), axis=0, keepdims=True).astype(jnp.int32)
    slot_table = one_hot(dest[...] * STRIDE + rank, slots).astype(BF)
    block_table = one_hot(cut_col[...], width).astype(BF)
    chosen = dot(slot_table, block_table, (1, 1))

    line = lax.broadcasted_iota(jnp.int32, (GROUP, width), 0)
    masks = [jnp.where(line == k, 1.0, 0.0).astype(BF) for k in range(GROUP)]

    def forward(ref, rows_at):
        parts = []
        for g in range(count // GROUP):
            rows = rows_at(g)
            left = jnp.concatenate([rows * m for m in masks], axis=1)
            block = ref[0, g * GROUP : (g + 1) * GROUP].reshape(GROUP * width, width)
            parts.append(dot(left, block, (1, 0)))
        return jnp.concatenate(parts, axis=0)

    def backward(ref, vectors):
        parts = []
        for g in range(count // GROUP):
            rows = vectors[g * GROUP : (g + 1) * GROUP]
            total = jnp.zeros((GROUP, width), F32)
            for k in range(GROUP):
                total = total + dot(rows * masks[k], ref[0, g * GROUP + k], (1, 1))
            parts.append(total)
        return jnp.concatenate(parts, axis=0)

    def wait_all(buffer, number, sem):
        piece = buffer.at[pl.ds(0, number)]
        pltpu.make_async_copy(piece, piece, sem).wait()

    def send_cut(turn, w, stats):
        wb = jnp.broadcast_to(w, (GROUP, width)).astype(BF)
        products = forward(cuts, lambda g: wb)
        send_a[turn, :, :STRIDE] = spread(slot_table, products, (1, 0)).reshape(
            owners, STRIDE, width
        )
        send_a[turn, :, STRIDE:] = stats
        recv_a[turn, flat] = send_a[turn, c]

        def go(k, carry):
            other = lax.rem(flat + k, n_dev)
            oc, orow = lax.rem(other, owners), other // owners
            pltpu.make_async_remote_copy(
                src_ref=send_a.at[turn, oc],
                dst_ref=recv_a.at[turn, flat],
                send_sem=sem_a.at[0, turn],
                recv_sem=sem_a.at[1, turn],
                device_id={"col": oc, "row": orow},
                device_id_type=MESH,
            ).start()
            return carry

        lax.fori_loop(1, n_dev, go, 0)

    def send_rows(turn, y, moved):
        yg = dot(row_table, y.astype(BF), (0, 0)).astype(BF)
        products = forward(tiles, lambda g: yg[g * GROUP : (g + 1) * GROUP])
        send_r[turn, :blocks] = spread(col_table, products, (1, 0))
        send_r[turn, blocks:] = moved
        recv_r[turn, r] = send_r[turn]

        def go(k, carry):
            pltpu.make_async_remote_copy(
                src_ref=send_r.at[turn],
                dst_ref=recv_r.at[turn, r],
                send_sem=sem_r.at[0, turn],
                recv_sem=sem_r.at[1, turn],
                device_id={"col": c, "row": lax.rem(r + k, n_row)},
                device_id_type=MESH,
            ).start()
            return carry

        lax.fori_loop(1, n_row, go, 0)

    def to_columns(source, dest_ref, sems, turn):
        def go(k, carry):
            oc = lax.rem(c + k, owners)
            pltpu.make_async_remote_copy(
                src_ref=source(oc),
                dst_ref=dest_ref.at[turn, c],
                send_sem=sems.at[0, turn],
                recv_sem=sems.at[1, turn],
                device_id={"col": oc, "row": r},
                device_id_type=MESH,
            ).start()
            return carry

        lax.fori_loop(1, owners, go, 0)

    x, y, w = x0[...], y0[...], w0[...]
    pl.semaphore_wait(barrier, n_dev - 1)
    send_cut(0, w, chosen.reshape(owners, STRIDE, width))
    send_rows(0, y, jnp.zeros((STRIDE, width), F32))

    eta = jnp.full((1, 1), step[0], F32)
    omega = jnp.full((1, 1), weight[0], F32)
    held = None
    for turn in range(ITERS + 1):
        wait_all(recv_a.at[turn], n_dev - 1, sem_a.at[1, turn])
        if turn == 0:
            held = recv_a[0, :, STRIDE:].reshape(n_dev * STRIDE, width).astype(BF)
        prices = recv_a[turn, :, :STRIDE].reshape(n_dev * STRIDE, width)
        cut_part = spread(held, prices, (0, 0))[:blocks]
        wait_all(recv_r.at[turn], n_row - 1, sem_r.at[1, turn])
        from_rows = recv_r[turn, 0]
        for other in range(1, n_row):
            from_rows = from_rows + recv_r[turn, other]
        grad = cost[...] + (cut_part - from_rows[:blocks])
        if turn == 1:
            stats = jnp.sum(recv_a[turn, :, STRIDE:], axis=0)
            moved = jnp.sum(stats[:1], axis=1, keepdims=True)
            dual_moved = jnp.sum(
                stats[1:2] + jnp.sum(from_rows[blocks:], axis=0, keepdims=True),
                axis=1,
                keepdims=True,
            )
            omega = jnp.sqrt(omega * jnp.sqrt((moved + EPSILON) / (dual_moved + EPSILON)))
        if turn == ITERS:
            break
        tau = eta / omega
        sigma = eta * omega
        new_x = jnp.clip(x - tau * grad, 0.0, 1.0)
        xbar = (2.0 * new_x - x).astype(BF)

        mine = (
            recv_a[0, pl.ds(r * owners, owners), STRIDE:].reshape(slots, width)[:, :blocks].astype(BF)
        )
        send_x[turn] = dot(mine, xbar, (1, 0)).reshape(owners, STRIDE, width)
        recv_x[turn, c] = send_x[turn, c]
        to_columns(lambda oc: send_x.at[turn, oc], recv_x, sem_x, turn)

        xg = dot(col_table, xbar, (0, 0)).astype(BF)
        send_p[turn] = spread(row_table, backward(tiles, xg), (1, 0))
        recv_p[turn, c] = send_p[turn]
        to_columns(lambda oc: send_p.at[turn], recv_p, sem_p, turn)

        wait_all(recv_x.at[turn], owners - 1, sem_x.at[1, turn])
        xr = recv_x[turn].reshape(slots, width).astype(BF)
        xk = dot(slot_table, xr, (0, 0)).astype(BF)
        activity = jnp.sum(backward(cuts, xk), axis=0, keepdims=True)
        new_w = jnp.maximum(w + sigma * (activity - 1.0), 0.0)
        place = lax.broadcasted_iota(jnp.int32, (STRIDE, width), 0)
        step_x = jnp.where(r == 0, 1.0, 0.0) * (new_x - x)
        step_w = new_w - w
        stats = jnp.where(
            place == 0,
            jnp.sum(step_x * step_x, axis=0, keepdims=True),
            jnp.where(place == 1, step_w * step_w, 0.0),
        )
        send_cut(turn + 1, new_w, jnp.broadcast_to(stats[None], (owners, STRIDE, width)))

        wait_all(recv_p.at[turn], owners - 1, sem_p.at[1, turn])
        total = jnp.sum(recv_p[turn], axis=0)
        new_y = jnp.maximum(y + sigma * (demand[...] - total), 0.0)
        step_y = new_y - y
        squares = jnp.sum((step_y * step_y).reshape(row_blocks // STRIDE, STRIDE, width), axis=0)
        send_rows(turn + 1, new_y, squares)
        x, y, w = new_x, new_y, new_w

    x_out[...] = x
    y_out[...] = y
    w_out[...] = w
    here = lax.broadcasted_iota(jnp.int32, (blocks, blocks), 0) == lax.broadcasted_iota(
        jnp.int32, (blocks, blocks), 1
    )
    power = jnp.exp2(exps[...].astype(F32))
    limit = -0.125 * jnp.sum(jnp.where(here, power, 0.0), axis=1, keepdims=True)
    v_out[...] = jnp.maximum(limit - grad, 0.0)

    for turn in range(ITERS + 1):
        wait_all(recv_a.at[turn], n_dev - 1, sem_a.at[0, turn])
        wait_all(recv_r.at[turn], n_row - 1, sem_r.at[0, turn])
        if turn < ITERS:
            wait_all(recv_x.at[turn], owners - 1, sem_x.at[0, turn])
            wait_all(recv_p.at[turn], owners - 1, sem_p.at[0, turn])


def local(
    covering_tiles,
    tile_row_blocks,
    tile_cols,
    cut_tiles,
    cut_dest,
    cut_cols,
    cost,
    demand,
    primal_start,
    initial_duals,
    cut_start,
    primal_weight,
    step_size,
    exponents,
    owners,
    n_row,
):
    blocks, width = cost.shape
    row_blocks = demand.shape[0]
    n_dev = owners * n_row
    phases = ITERS + 1
    vmem = pl.BlockSpec(memory_space=pltpu.VMEM)
    smem = pl.BlockSpec(memory_space=pltpu.SMEM)
    return pl.pallas_call(
        functools.partial(kernel, owners, n_row),
        out_shape=(
            jax.ShapeDtypeStruct(primal_start.shape, F32),
            jax.ShapeDtypeStruct(initial_duals.shape, F32),
            jax.ShapeDtypeStruct(cut_start.shape, F32),
            jax.ShapeDtypeStruct(cost.shape, F32),
        ),
        in_specs=[vmem] * 11 + [smem] * 2 + [vmem],
        out_specs=(vmem,) * 4,
        scratch_shapes=[
            pltpu.VMEM((phases, owners, 2 * STRIDE, width), F32),
            pltpu.VMEM((phases, n_dev, 2 * STRIDE, width), F32),
            pltpu.VMEM((ITERS, owners, STRIDE, width), F32),
            pltpu.VMEM((ITERS, owners, STRIDE, width), F32),
            pltpu.VMEM((ITERS, row_blocks, width), F32),
            pltpu.VMEM((ITERS, owners, row_blocks, width), F32),
            pltpu.VMEM((phases, blocks + STRIDE, width), F32),
            pltpu.VMEM((phases, n_row, blocks + STRIDE, width), F32),
            pltpu.SemaphoreType.DMA((2, phases)),
            pltpu.SemaphoreType.DMA((2, ITERS)),
            pltpu.SemaphoreType.DMA((2, ITERS)),
            pltpu.SemaphoreType.DMA((2, phases)),
        ],
        compiler_params=pltpu.CompilerParams(
            collective_id=0, has_side_effects=True, vmem_limit_bytes=44 * 1024 * 1024
        ),
        name="pdhg",
    )(
        covering_tiles,
        tile_row_blocks,
        tile_cols,
        cut_tiles,
        cut_dest.reshape(cut_cols.shape),
        cut_cols,
        cost,
        demand,
        primal_start,
        initial_duals,
        cut_start,
        primal_weight,
        step_size,
        exponents.reshape(1, blocks),
    )


def solution(mesh):
    in_specs = (
        P("row", "col", None, None),
        P("row", "col"),
        P("row", "col"),
        P("col", "row", None, None),
        P("col", "row", None),
        P("col", "row"),
        P("col", None),
        P("row", None),
        P("col", None),
        P("row", None),
        P("col", "row"),
        P(),
        P(),
        P("col"),
    )
    out_specs = (P("col", None), P("row", None), P("col", "row"), P("col", None))
    body = functools.partial(local, owners=mesh.shape["col"], n_row=mesh.shape["row"])
    return jax.shard_map(body, mesh=mesh, in_specs=in_specs, out_specs=out_specs, check_vma=False)
```

```python
import functools

import jax
import jax.numpy as jnp
from jax import lax
from jax.experimental import pallas as pl
from jax.experimental.pallas import tpu as pltpu
from jax.sharding import PartitionSpec as P

ITERS = 2
EPSILON = 1e-06
GROUP = 16
STRIDE = 8
BF = jnp.bfloat16
F32 = jnp.float32
MESH = pl.DeviceIdType.MESH


def dot(a, b, contract):
    return lax.dot_general(a, b, ((contract[:1], contract[1:]), ((), ())), preferred_element_type=F32)


def split3(values):
    high = values.astype(BF)
    rest = values - high.astype(F32)
    middle = rest.astype(BF)
    low = (rest - middle.astype(F32)).astype(BF)
    return high, middle, low


def spread(table, values, contract):
    high, middle, low = split3(values)
    return dot(table, high, contract) + (dot(table, middle, contract) + dot(table, low, contract))


def kernel(
    owners,
    n_row,
    far_dest,
    far_cut_col,
    far_w0,
    far_cuts,
    far_row_of,
    far_y0,
    far_tiles,
    far_col_of,
    far_x0,
    far_cost,
    far_demand,
    far_exps,
    weight,
    step,
    x_out,
    y_out,
    w_out,
    v_out,
    send_a,
    recv_a,
    send_x,
    recv_x,
    send_p,
    recv_p,
    send_r,
    recv_r,
    dest,
    cut_col,
    w0,
    cuts,
    row_of,
    y0,
    tiles,
    col_of,
    x0,
    cost,
    demand,
    exps,
    sem_in,
    sem_a,
    sem_x,
    sem_p,
    sem_r,
):
    far = (far_dest, far_cut_col, far_w0, far_cuts, far_row_of, far_y0)
    far += (far_tiles, far_col_of, far_x0, far_cost, far_demand, far_exps)
    near = (dest, cut_col, w0, cuts, row_of, y0, tiles, col_of, x0, cost, demand, exps)
    loads = [pltpu.make_async_copy(a, b, sem_in.at[i]) for i, (a, b) in enumerate(zip(far, near))]
    for load in loads:
        load.start()
    c = lax.axis_index("col")
    r = lax.axis_index("row")
    n_dev = owners * n_row
    flat = r * owners + c
    count = tiles.shape[1]
    blocks, width = cost.shape
    row_blocks = demand.shape[0]
    slots = owners * STRIDE

    barrier = pltpu.get_barrier_semaphore()

    def greet(k, carry):
        other = lax.rem(flat + k, n_dev)
        pl.semaphore_signal(
            barrier,
            inc=1,
            device_id={"col": lax.rem(other, owners), "row": other // owners},
            device_id_type=MESH,
        )
        return carry

    lax.fori_loop(1, n_dev, greet, 0)

    for load in loads[:4]:
        load.wait()

    def one_hot(row, size):
        return jnp.where(
            lax.broadcasted_iota(jnp.int32, (size, row.shape[1]), 0) == row, 1.0, 0.0
        )

    owner_table = one_hot(dest[...], max(owners, 16)).astype(BF)
    same = dot(owner_table, owner_table, (0, 0))
    earlier = lax.broadcasted_iota(jnp.int32, same.shape, 0) < lax.broadcasted_iota(
        jnp.int32, same.shape, 1
    )
    rank = jnp.sum(jnp.where(earlier, same, 0.0), axis=0, keepdims=True).astype(jnp.int32)
    slot_table = one_hot(dest[...] * STRIDE + rank, slots).astype(BF)
    block_table = one_hot(cut_col[...], width).astype(BF)
    chosen = dot(slot_table, block_table, (1, 1))

    line = lax.broadcasted_iota(jnp.int32, (GROUP, width), 0)
    masks = [jnp.where(line == k, 1.0, 0.0).astype(BF) for k in range(GROUP)]

    def forward(ref, rows_at):
        parts = []
        for g in range(count // GROUP):
            rows = rows_at(g)
            left = jnp.concatenate([rows * m for m in masks], axis=1)
            block = ref[0, g * GROUP : (g + 1) * GROUP].reshape(GROUP * width, width)
            parts.append(dot(left, block, (1, 0)))
        return jnp.concatenate(parts, axis=0)

    def backward(ref, vectors):
        parts = []
        for g in range(count // GROUP):
            rows = vectors[g * GROUP : (g + 1) * GROUP]
            block = ref[0, g * GROUP : (g + 1) * GROUP].reshape(GROUP * width, width)
            every = dot(rows, block, (1, 1))
            total = jnp.zeros((GROUP, width), F32)
            for k in range(GROUP):
                total = jnp.where(line == k, every[:, k * width : (k + 1) * width], total)
            parts.append(total)
        return jnp.concatenate(parts, axis=0)

    def wait_all(buffer, number, sem):
        piece = buffer.at[pl.ds(0, number)]
        pltpu.make_async_copy(piece, piece, sem).wait()

    def send_cut(turn, w, stats):
        wb = jnp.broadcast_to(w, (GROUP, width)).astype(BF)
        products = forward(cuts, lambda g: wb)
        send_a[turn, :, :STRIDE] = spread(slot_table, products, (1, 0)).reshape(
            owners, STRIDE, width
        )
        send_a[turn, :, STRIDE:] = stats
        recv_a[turn, flat] = send_a[turn, c]
        if turn == 0:
            pl.semaphore_wait(barrier, n_dev - 1)

        def go(k, carry):
            other = lax.rem(flat + k, n_dev)
            oc, orow = lax.rem(other, owners), other // owners
            pltpu.make_async_remote_copy(
                src_ref=send_a.at[turn, oc],
                dst_ref=recv_a.at[turn, flat],
                send_sem=sem_a.at[0, turn],
                recv_sem=sem_a.at[1, turn],
                device_id={"col": oc, "row": orow},
                device_id_type=MESH,
            ).start()
            return carry

        lax.fori_loop(1, n_dev, go, 0)

    def send_rows(turn, y, moved):
        yg = dot(row_table, y.astype(BF), (0, 0)).astype(BF)
        products = forward(tiles, lambda g: yg[g * GROUP : (g + 1) * GROUP])
        send_r[turn, :blocks] = spread(col_table, products, (1, 0))
        send_r[turn, blocks:] = moved
        recv_r[turn, r] = send_r[turn]

        def go(k, carry):
            pltpu.make_async_remote_copy(
                src_ref=send_r.at[turn],
                dst_ref=recv_r.at[turn, r],
                send_sem=sem_r.at[0, turn],
                recv_sem=sem_r.at[1, turn],
                device_id={"col": c, "row": lax.rem(r + k, n_row)},
                device_id_type=MESH,
            ).start()
            return carry

        lax.fori_loop(1, n_row, go, 0)

    def to_columns(source, dest_ref, sems, turn):
        def go(k, carry):
            oc = lax.rem(c + k, owners)
            pltpu.make_async_remote_copy(
                src_ref=source(oc),
                dst_ref=dest_ref.at[turn, c],
                send_sem=sems.at[0, turn],
                recv_sem=sems.at[1, turn],
                device_id={"col": oc, "row": r},
                device_id_type=MESH,
            ).start()
            return carry

        lax.fori_loop(1, owners, go, 0)

    w = w0[...]
    send_cut(0, w, chosen.reshape(owners, STRIDE, width))
    for load in loads[4:]:
        load.wait()
    row_table = one_hot(row_of[...], row_blocks).astype(BF)
    col_table = one_hot(col_of[...], blocks).astype(BF)
    x, y = x0[...], y0[...]
    send_rows(0, y, jnp.zeros((STRIDE, width), F32))

    eta = jnp.full((1, 1), step[0], F32)
    omega = jnp.full((1, 1), weight[0], F32)
    held = None
    for turn in range(ITERS + 1):
        wait_all(recv_a.at[turn], n_dev - 1, sem_a.at[1, turn])
        if turn == 0:
            held = recv_a[0, :, STRIDE:].reshape(n_dev * STRIDE, width).astype(BF)
        prices = recv_a[turn, :, :STRIDE].reshape(n_dev * STRIDE, width)
        cut_part = spread(held, prices, (0, 0))[:blocks]
        wait_all(recv_r.at[turn], n_row - 1, sem_r.at[1, turn])
        from_rows = recv_r[turn, 0]
        for other in range(1, n_row):
            from_rows = from_rows + recv_r[turn, other]
        grad = cost[...] + (cut_part - from_rows[:blocks])
        if turn == 1:
            stats = jnp.sum(recv_a[turn, :, STRIDE:], axis=0)
            moved = jnp.sum(stats[:1], axis=1, keepdims=True)
            dual_moved = jnp.sum(
                stats[1:2] + jnp.sum(from_rows[blocks:], axis=0, keepdims=True),
                axis=1,
                keepdims=True,
            )
            omega = jnp.sqrt(omega * jnp.sqrt((moved + EPSILON) / (dual_moved + EPSILON)))
        if turn == ITERS:
            break
        tau = eta / omega
        sigma = eta * omega
        new_x = jnp.clip(x - tau * grad, 0.0, 1.0)
        xbar = (2.0 * new_x - x).astype(BF)

        mine = (
            recv_a[0, pl.ds(r * owners, owners), STRIDE:].reshape(slots, width)[:, :blocks].astype(BF)
        )
        send_x[turn] = dot(mine, xbar, (1, 0)).reshape(owners, STRIDE, width)
        recv_x[turn, c] = send_x[turn, c]
        to_columns(lambda oc: send_x.at[turn, oc], recv_x, sem_x, turn)

        xg = dot(col_table, xbar, (0, 0)).astype(BF)
        send_p[turn] = spread(row_table, backward(tiles, xg), (1, 0))
        recv_p[turn, c] = send_p[turn]
        to_columns(lambda oc: send_p.at[turn], recv_p, sem_p, turn)

        wait_all(recv_x.at[turn], owners - 1, sem_x.at[1, turn])
        xr = recv_x[turn].reshape(slots, width).astype(BF)
        xk = dot(slot_table, xr, (0, 0)).astype(BF)
        activity = jnp.sum(backward(cuts, xk), axis=0, keepdims=True)
        new_w = jnp.maximum(w + sigma * (activity - 1.0), 0.0)
        place = lax.broadcasted_iota(jnp.int32, (STRIDE, width), 0)
        step_x = jnp.where(r == 0, 1.0, 0.0) * (new_x - x)
        step_w = new_w - w
        stats = jnp.where(
            place == 0,
            jnp.sum(step_x * step_x, axis=0, keepdims=True),
            jnp.where(place == 1, step_w * step_w, 0.0),
        )
        send_cut(turn + 1, new_w, jnp.broadcast_to(stats[None], (owners, STRIDE, width)))

        wait_all(recv_p.at[turn], owners - 1, sem_p.at[1, turn])
        total = jnp.sum(recv_p[turn], axis=0)
        new_y = jnp.maximum(y + sigma * (demand[...] - total), 0.0)
        step_y = new_y - y
        squares = jnp.sum((step_y * step_y).reshape(row_blocks // STRIDE, STRIDE, width), axis=0)
        send_rows(turn + 1, new_y, squares)
        x, y, w = new_x, new_y, new_w

    x_out[...] = x
    y_out[...] = y
    w_out[...] = w
    here = lax.broadcasted_iota(jnp.int32, (blocks, blocks), 0) == lax.broadcasted_iota(
        jnp.int32, (blocks, blocks), 1
    )
    power = jnp.exp2(exps[...].astype(F32))
    limit = -0.125 * jnp.sum(jnp.where(here, power, 0.0), axis=1, keepdims=True)
    v_out[...] = jnp.maximum(limit - grad, 0.0)

    for turn in range(ITERS + 1):
        wait_all(recv_a.at[turn], n_dev - 1, sem_a.at[0, turn])
        wait_all(recv_r.at[turn], n_row - 1, sem_r.at[0, turn])
        if turn < ITERS:
            wait_all(recv_x.at[turn], owners - 1, sem_x.at[0, turn])
            wait_all(recv_p.at[turn], owners - 1, sem_p.at[0, turn])


def local(
    covering_tiles,
    tile_row_blocks,
    tile_cols,
    cut_tiles,
    cut_dest,
    cut_cols,
    cost,
    demand,
    primal_start,
    initial_duals,
    cut_start,
    primal_weight,
    step_size,
    exponents,
    owners,
    n_row,
):
    blocks, width = cost.shape
    row_blocks = demand.shape[0]
    n_dev = owners * n_row
    phases = ITERS + 1
    vmem = pl.BlockSpec(memory_space=pltpu.VMEM)
    smem = pl.BlockSpec(memory_space=pltpu.SMEM)
    operands = (
        cut_dest.reshape(cut_cols.shape),
        cut_cols,
        cut_start,
        cut_tiles,
        tile_row_blocks,
        initial_duals,
        covering_tiles,
        tile_cols,
        primal_start,
        cost,
        demand,
        exponents.reshape(1, blocks),
    )
    return pl.pallas_call(
        functools.partial(kernel, owners, n_row),
        out_shape=(
            jax.ShapeDtypeStruct(primal_start.shape, F32),
            jax.ShapeDtypeStruct(initial_duals.shape, F32),
            jax.ShapeDtypeStruct(cut_start.shape, F32),
            jax.ShapeDtypeStruct(cost.shape, F32),
        ),
        in_specs=[pl.BlockSpec(memory_space=pltpu.HBM)] * 12 + [smem] * 2,
        out_specs=(vmem,) * 4,
        scratch_shapes=[
            pltpu.VMEM((phases, owners, 2 * STRIDE, width), F32),
            pltpu.VMEM((phases, n_dev, 2 * STRIDE, width), F32),
            pltpu.VMEM((ITERS, owners, STRIDE, width), F32),
            pltpu.VMEM((ITERS, owners, STRIDE, width), F32),
            pltpu.VMEM((ITERS, row_blocks, width), F32),
            pltpu.VMEM((ITERS, owners, row_blocks, width), F32),
            pltpu.VMEM((phases, blocks + STRIDE, width), F32),
            pltpu.VMEM((phases, n_row, blocks + STRIDE, width), F32),
            *[pltpu.VMEM(a.shape, a.dtype) for a in operands],
            pltpu.SemaphoreType.DMA((len(operands),)),
            pltpu.SemaphoreType.DMA((2, phases)),
            pltpu.SemaphoreType.DMA((2, ITERS)),
            pltpu.SemaphoreType.DMA((2, ITERS)),
            pltpu.SemaphoreType.DMA((2, phases)),
        ],
        compiler_params=pltpu.CompilerParams(
            collective_id=0, has_side_effects=True, vmem_limit_bytes=44 * 1024 * 1024
        ),
        name="pdhg",
    )(*operands, primal_weight, step_size)


def solution(mesh):
    in_specs = (
        P("row", "col", None, None),
        P("row", "col"),
        P("row", "col"),
        P("col", "row", None, None),
        P("col", "row", None),
        P("col", "row"),
        P("col", None),
        P("row", None),
        P("col", None),
        P("row", None),
        P("col", "row"),
        P(),
        P(),
        P("col"),
    )
    out_specs = (P("col", None), P("row", None), P("col", "row"), P("col", None))
    body = functools.partial(local, owners=mesh.shape["col"], n_row=mesh.shape["row"])
    return jax.shard_map(body, mesh=mesh, in_specs=in_specs, out_specs=out_specs, check_vma=False)
```

```python
import functools

import jax
import jax.numpy as jnp
from jax import lax
from jax.experimental import pallas as pl
from jax.experimental.pallas import tpu as pltpu
from jax.sharding import PartitionSpec as P

ITERS = 2
EPSILON = 1e-06
GROUP = 16
STRIDE = 8
BF = jnp.bfloat16
F32 = jnp.float32
MESH = pl.DeviceIdType.MESH


def dot(a, b, contract):
    return lax.dot_general(a, b, ((contract[:1], contract[1:]), ((), ())), preferred_element_type=F32)


def split3(values):
    high = values.astype(BF)
    rest = values - high.astype(F32)
    middle = rest.astype(BF)
    low = (rest - middle.astype(F32)).astype(BF)
    return high, middle, low


def spread(table, values, contract):
    high, middle, low = split3(values)
    return dot(table, high, contract) + (dot(table, middle, contract) + dot(table, low, contract))


def kernel(
    owners,
    n_row,
    far_dest,
    far_cut_col,
    far_w0,
    far_cuts,
    far_row_of,
    far_y0,
    far_tiles,
    far_col_of,
    far_x0,
    far_cost,
    far_demand,
    far_exps,
    weight,
    step,
    x_out,
    y_out,
    w_out,
    v_out,
    send_a,
    recv_a,
    send_x,
    recv_x,
    send_p,
    recv_p,
    send_r,
    recv_r,
    dest,
    cut_col,
    w0,
    cuts,
    row_of,
    y0,
    tiles,
    col_of,
    x0,
    cost,
    demand,
    exps,
    sem_in,
    sem_a,
    sem_x,
    sem_p,
    sem_r,
):
    far = (far_dest, far_cut_col, far_w0, far_cuts, far_row_of, far_y0)
    far += (far_tiles, far_col_of, far_x0, far_cost, far_demand, far_exps)
    near = (dest, cut_col, w0, cuts, row_of, y0, tiles, col_of, x0, cost, demand, exps)
    loads = [pltpu.make_async_copy(a, b, sem_in.at[i]) for i, (a, b) in enumerate(zip(far, near))]
    for load in loads:
        load.start()
    c = lax.axis_index("col")
    r = lax.axis_index("row")
    n_dev = owners * n_row
    flat = r * owners + c
    count = tiles.shape[1]
    blocks, width = cost.shape
    row_blocks = demand.shape[0]
    slots = owners * STRIDE

    barrier = pltpu.get_barrier_semaphore()

    def greet(k, carry):
        other = lax.rem(flat + k, n_dev)
        pl.semaphore_signal(
            barrier,
            inc=1,
            device_id={"col": lax.rem(other, owners), "row": other // owners},
            device_id_type=MESH,
        )
        return carry

    lax.fori_loop(1, n_dev, greet, 0)

    for load in loads[:4]:
        load.wait()

    def one_hot(row, size):
        return jnp.where(
            lax.broadcasted_iota(jnp.int32, (size, row.shape[1]), 0) == row, 1.0, 0.0
        )

    owner_table = one_hot(dest[...], max(owners, 16)).astype(BF)
    same = dot(owner_table, owner_table, (0, 0))
    earlier = lax.broadcasted_iota(jnp.int32, same.shape, 0) < lax.broadcasted_iota(
        jnp.int32, same.shape, 1
    )
    rank = jnp.sum(jnp.where(earlier, same, 0.0), axis=0, keepdims=True).astype(jnp.int32)
    slot_table = one_hot(dest[...] * STRIDE + rank, slots).astype(BF)
    block_table = one_hot(cut_col[...], width).astype(BF)
    chosen = dot(slot_table, block_table, (1, 1))

    line = lax.broadcasted_iota(jnp.int32, (GROUP, width), 0)
    masks = [jnp.where(line == k, 1.0, 0.0).astype(BF) for k in range(GROUP)]

    def forward(ref, rows_at):
        parts = []
        for g in range(count // GROUP):
            rows = rows_at(g)
            left = jnp.concatenate([rows * m for m in masks], axis=1)
            block = ref[0, g * GROUP : (g + 1) * GROUP].reshape(GROUP * width, width)
            parts.append(dot(left, block, (1, 0)))
        return jnp.concatenate(parts, axis=0)

    def backward(ref, vectors):
        parts = []
        for g in range(count // GROUP):
            rows = vectors[g * GROUP : (g + 1) * GROUP]
            block = ref[0, g * GROUP : (g + 1) * GROUP].reshape(GROUP * width, width)
            every = dot(rows, block, (1, 1))
            total = jnp.zeros((GROUP, width), F32)
            for k in range(GROUP):
                total = jnp.where(line == k, every[:, k * width : (k + 1) * width], total)
            parts.append(total)
        return jnp.concatenate(parts, axis=0)

    def wait_all(buffer, number, sem):
        piece = buffer.at[pl.ds(0, number)]
        pltpu.make_async_copy(piece, piece, sem).wait()

    def send_cut(turn, w, stats):
        wb = jnp.broadcast_to(w, (GROUP, width)).astype(BF)
        products = forward(cuts, lambda g: wb)
        placed = spread(slot_table, products, (1, 0)).reshape(owners, STRIDE, width)
        if stats is None:
            stats = placed - placed.astype(BF).astype(F32)
        send_a[turn] = jnp.concatenate([placed, stats], axis=1).astype(BF)
        recv_a[turn, flat] = send_a[turn, c]
        if turn == 0:
            pl.semaphore_wait(barrier, n_dev - 1)

        def go(k, carry):
            other = lax.rem(flat + k, n_dev)
            oc, orow = lax.rem(other, owners), other // owners
            pltpu.make_async_remote_copy(
                src_ref=send_a.at[turn, oc],
                dst_ref=recv_a.at[turn, flat],
                send_sem=sem_a.at[0, turn],
                recv_sem=sem_a.at[1, turn],
                device_id={"col": oc, "row": orow},
                device_id_type=MESH,
            ).start()
            return carry

        lax.fori_loop(1, n_dev, go, 0)

    def send_rows(turn, y, moved):
        yg = dot(row_table, y.astype(BF), (0, 0)).astype(BF)
        products = forward(tiles, lambda g: yg[g * GROUP : (g + 1) * GROUP])
        send_r[turn, :blocks] = spread(col_table, products, (1, 0))
        send_r[turn, blocks:] = moved
        recv_r[turn, r] = send_r[turn]

        def go(k, carry):
            pltpu.make_async_remote_copy(
                src_ref=send_r.at[turn],
                dst_ref=recv_r.at[turn, r],
                send_sem=sem_r.at[0, turn],
                recv_sem=sem_r.at[1, turn],
                device_id={"col": c, "row": lax.rem(r + k, n_row)},
                device_id_type=MESH,
            ).start()
            return carry

        lax.fori_loop(1, n_row, go, 0)

    def to_columns(source, dest_ref, sems, turn):
        def go(k, carry):
            oc = lax.rem(c + k, owners)
            pltpu.make_async_remote_copy(
                src_ref=source(oc),
                dst_ref=dest_ref.at[turn, c],
                send_sem=sems.at[0, turn],
                recv_sem=sems.at[1, turn],
                device_id={"col": oc, "row": r},
                device_id_type=MESH,
            ).start()
            return carry

        lax.fori_loop(1, owners, go, 0)

    w = w0[...]
    send_cut(0, w, chosen.reshape(owners, STRIDE, width))
    for load in loads[4:]:
        load.wait()
    row_table = one_hot(row_of[...], row_blocks).astype(BF)
    col_table = one_hot(col_of[...], blocks).astype(BF)
    x, y = x0[...], y0[...]
    send_rows(0, y, jnp.zeros((STRIDE, width), F32))

    eta = jnp.full((1, 1), step[0], F32)
    omega = jnp.full((1, 1), weight[0], F32)
    held = None
    for turn in range(ITERS + 1):
        wait_all(recv_a.at[turn], n_dev - 1, sem_a.at[1, turn])
        landed = recv_a[turn].astype(F32)
        prices = landed[:, :STRIDE].reshape(n_dev * STRIDE, width).astype(BF)
        beside = landed[:, STRIDE:]
        if turn == 0:
            held = beside.reshape(n_dev * STRIDE, width).astype(BF)
        cut_part = dot(held, prices, (0, 0))
        if turn == ITERS:
            low = beside.reshape(n_dev * STRIDE, width).astype(BF)
            cut_part = cut_part + dot(held, low, (0, 0))
        cut_part = cut_part[:blocks]
        wait_all(recv_r.at[turn], n_row - 1, sem_r.at[1, turn])
        from_rows = recv_r[turn, 0]
        for other in range(1, n_row):
            from_rows = from_rows + recv_r[turn, other]
        grad = cost[...] + (cut_part - from_rows[:blocks])
        if turn == 1:
            stats = jnp.sum(beside, axis=0)
            moved = jnp.sum(stats[0:1] + stats[1:2] + stats[2:3], axis=1, keepdims=True)
            dual_moved = jnp.sum(
                (stats[3:4] + stats[4:5] + stats[5:6])
                + jnp.sum(from_rows[blocks:], axis=0, keepdims=True),
                axis=1,
                keepdims=True,
            )
            omega = jnp.sqrt(omega * jnp.sqrt((moved + EPSILON) / (dual_moved + EPSILON)))
        if turn == ITERS:
            break
        tau = eta / omega
        sigma = eta * omega
        new_x = jnp.clip(x - tau * grad, 0.0, 1.0)
        xbar = (2.0 * new_x - x).astype(BF)

        mine = (
            recv_a[0, pl.ds(r * owners, owners)]
            .astype(F32)[:, STRIDE:]
            .reshape(slots, width)[:, :blocks]
            .astype(BF)
        )
        send_x[turn] = dot(mine, xbar, (1, 0)).reshape(owners, STRIDE, width)
        recv_x[turn, c] = send_x[turn, c]
        to_columns(lambda oc: send_x.at[turn, oc], recv_x, sem_x, turn)

        xg = dot(col_table, xbar, (0, 0)).astype(BF)
        send_p[turn] = spread(row_table, backward(tiles, xg), (1, 0)).astype(BF)
        recv_p[turn, c] = send_p[turn]
        to_columns(lambda oc: send_p.at[turn], recv_p, sem_p, turn)

        wait_all(recv_x.at[turn], owners - 1, sem_x.at[1, turn])
        xr = recv_x[turn].reshape(slots, width).astype(BF)
        xk = dot(slot_table, xr, (0, 0)).astype(BF)
        activity = jnp.sum(backward(cuts, xk), axis=0, keepdims=True)
        new_w = jnp.maximum(w + sigma * (activity - 1.0), 0.0)
        place = lax.broadcasted_iota(jnp.int32, (STRIDE, width), 0)
        step_x = jnp.where(r == 0, 1.0, 0.0) * (new_x - x)
        step_w = new_w - w
        stats = None
        if turn + 1 < ITERS:
            pieces = split3(jnp.sum(step_x * step_x, axis=0, keepdims=True)) + split3(step_w * step_w)
            stats = jnp.zeros((STRIDE, width), F32)
            for at, piece in enumerate(pieces):
                stats = jnp.where(place == at, piece.astype(F32), stats)
            stats = jnp.broadcast_to(stats[None], (owners, STRIDE, width))
        send_cut(turn + 1, new_w, stats)

        wait_all(recv_p.at[turn], owners - 1, sem_p.at[1, turn])
        total = jnp.sum(recv_p[turn].astype(F32), axis=0)
        new_y = jnp.maximum(y + sigma * (demand[...] - total), 0.0)
        step_y = new_y - y
        squares = jnp.sum((step_y * step_y).reshape(row_blocks // STRIDE, STRIDE, width), axis=0)
        send_rows(turn + 1, new_y, squares)
        x, y, w = new_x, new_y, new_w

    x_out[...] = x
    y_out[...] = y
    w_out[...] = w
    here = lax.broadcasted_iota(jnp.int32, (blocks, blocks), 0) == lax.broadcasted_iota(
        jnp.int32, (blocks, blocks), 1
    )
    power = jnp.exp2(exps[...].astype(F32))
    limit = -0.125 * jnp.sum(jnp.where(here, power, 0.0), axis=1, keepdims=True)
    v_out[...] = jnp.maximum(limit - grad, 0.0)

    for turn in range(ITERS + 1):
        wait_all(recv_a.at[turn], n_dev - 1, sem_a.at[0, turn])
        wait_all(recv_r.at[turn], n_row - 1, sem_r.at[0, turn])
        if turn < ITERS:
            wait_all(recv_x.at[turn], owners - 1, sem_x.at[0, turn])
            wait_all(recv_p.at[turn], owners - 1, sem_p.at[0, turn])


def local(
    covering_tiles,
    tile_row_blocks,
    tile_cols,
    cut_tiles,
    cut_dest,
    cut_cols,
    cost,
    demand,
    primal_start,
    initial_duals,
    cut_start,
    primal_weight,
    step_size,
    exponents,
    owners,
    n_row,
):
    blocks, width = cost.shape
    row_blocks = demand.shape[0]
    n_dev = owners * n_row
    phases = ITERS + 1
    vmem = pl.BlockSpec(memory_space=pltpu.VMEM)
    smem = pl.BlockSpec(memory_space=pltpu.SMEM)
    operands = (
        cut_dest.reshape(cut_cols.shape),
        cut_cols,
        cut_start,
        cut_tiles,
        tile_row_blocks,
        initial_duals,
        covering_tiles,
        tile_cols,
        primal_start,
        cost,
        demand,
        exponents.reshape(1, blocks),
    )
    return pl.pallas_call(
        functools.partial(kernel, owners, n_row),
        out_shape=(
            jax.ShapeDtypeStruct(primal_start.shape, F32),
            jax.ShapeDtypeStruct(initial_duals.shape, F32),
            jax.ShapeDtypeStruct(cut_start.shape, F32),
            jax.ShapeDtypeStruct(cost.shape, F32),
        ),
        in_specs=[pl.BlockSpec(memory_space=pltpu.HBM)] * 12 + [smem] * 2,
        out_specs=(vmem,) * 4,
        scratch_shapes=[
            pltpu.VMEM((phases, owners, 2 * STRIDE, width), BF),
            pltpu.VMEM((phases, n_dev, 2 * STRIDE, width), BF),
            pltpu.VMEM((ITERS, owners, STRIDE, width), F32),
            pltpu.VMEM((ITERS, owners, STRIDE, width), F32),
            pltpu.VMEM((ITERS, row_blocks, width), BF),
            pltpu.VMEM((ITERS, owners, row_blocks, width), BF),
            pltpu.VMEM((phases, blocks + STRIDE, width), F32),
            pltpu.VMEM((phases, n_row, blocks + STRIDE, width), F32),
            *[pltpu.VMEM(a.shape, a.dtype) for a in operands],
            pltpu.SemaphoreType.DMA((len(operands),)),
            pltpu.SemaphoreType.DMA((2, phases)),
            pltpu.SemaphoreType.DMA((2, ITERS)),
            pltpu.SemaphoreType.DMA((2, ITERS)),
            pltpu.SemaphoreType.DMA((2, phases)),
        ],
        compiler_params=pltpu.CompilerParams(
            collective_id=0, has_side_effects=True, vmem_limit_bytes=64 * 1024 * 1024
        ),
        name="pdhg",
    )(*operands, primal_weight, step_size)


def solution(mesh):
    in_specs = (
        P("row", "col", None, None),
        P("row", "col"),
        P("row", "col"),
        P("col", "row", None, None),
        P("col", "row", None),
        P("col", "row"),
        P("col", None),
        P("row", None),
        P("col", None),
        P("row", None),
        P("col", "row"),
        P(),
        P(),
        P("col"),
    )
    out_specs = (P("col", None), P("row", None), P("col", "row"), P("col", None))
    body = functools.partial(local, owners=mesh.shape["col"], n_row=mesh.shape["row"])
    return jax.shard_map(body, mesh=mesh, in_specs=in_specs, out_specs=out_specs, check_vma=False)
```

```python
import functools

import jax
import jax.numpy as jnp
from jax import lax
from jax.experimental import pallas as pl
from jax.experimental.pallas import tpu as pltpu
from jax.sharding import PartitionSpec as P

ITERS = 2
EPSILON = 1e-06
GROUP = 16
STRIDE = 8
BF = jnp.bfloat16
F32 = jnp.float32
MESH = pl.DeviceIdType.MESH


def dot(a, b, contract):
    return lax.dot_general(a, b, ((contract[:1], contract[1:]), ((), ())), preferred_element_type=F32)


def split3(values):
    high = values.astype(BF)
    rest = values - high.astype(F32)
    middle = rest.astype(BF)
    low = (rest - middle.astype(F32)).astype(BF)
    return high, middle, low


def spread(table, values, contract):
    high, middle, low = split3(values)
    return dot(table, high, contract) + (dot(table, middle, contract) + dot(table, low, contract))


def kernel(
    owners,
    n_row,
    far_dest,
    far_cut_col,
    far_w0,
    far_cuts,
    far_row_of,
    far_y0,
    far_tiles,
    far_col_of,
    far_x0,
    far_cost,
    far_demand,
    far_exps,
    weight,
    step,
    x_out,
    y_out,
    w_out,
    v_out,
    send_a,
    recv_a,
    send_x,
    recv_x,
    send_p,
    recv_p,
    send_r,
    recv_r,
    dest,
    cut_col,
    w0,
    cuts,
    row_of,
    y0,
    tiles,
    col_of,
    x0,
    cost,
    demand,
    exps,
    sem_in,
    sem_a,
    sem_x,
    sem_p,
    sem_r,
):
    far = (far_dest, far_cut_col, far_w0, far_cuts, far_row_of, far_y0)
    far += (far_tiles, far_col_of, far_x0, far_cost, far_demand, far_exps)
    near = (dest, cut_col, w0, cuts, row_of, y0, tiles, col_of, x0, cost, demand, exps)
    loads = [pltpu.make_async_copy(a, b, sem_in.at[i]) for i, (a, b) in enumerate(zip(far, near))]
    for load in loads:
        load.start()
    c = lax.axis_index("col")
    r = lax.axis_index("row")
    n_dev = owners * n_row
    flat = r * owners + c
    count = tiles.shape[1]
    blocks, width = cost.shape
    row_blocks = demand.shape[0]
    slots = owners * STRIDE

    barrier = pltpu.get_barrier_semaphore()

    def greet(k, carry):
        other = lax.rem(flat + k, n_dev)
        pl.semaphore_signal(
            barrier,
            inc=1,
            device_id={"col": lax.rem(other, owners), "row": other // owners},
            device_id_type=MESH,
        )
        return carry

    lax.fori_loop(1, n_dev, greet, 0)

    for load in loads[:4]:
        load.wait()

    def one_hot(row, size):
        return jnp.where(
            lax.broadcasted_iota(jnp.int32, (size, row.shape[1]), 0) == row, 1.0, 0.0
        )

    owner_table = one_hot(dest[...], max(owners, 16)).astype(BF)
    same = dot(owner_table, owner_table, (0, 0))
    earlier = lax.broadcasted_iota(jnp.int32, same.shape, 0) < lax.broadcasted_iota(
        jnp.int32, same.shape, 1
    )
    rank = jnp.sum(jnp.where(earlier, same, 0.0), axis=0, keepdims=True).astype(jnp.int32)
    slot_table = one_hot(dest[...] * STRIDE + rank, slots).astype(BF)
    block_table = one_hot(cut_col[...], width).astype(BF)
    chosen = dot(slot_table, block_table, (1, 1))

    line = lax.broadcasted_iota(jnp.int32, (GROUP, width), 0)
    masks = [jnp.where(line == k, 1.0, 0.0).astype(BF) for k in range(GROUP)]

    def forward(ref, rows_at):
        parts = []
        for g in range(count // GROUP):
            rows = rows_at(g)
            left = jnp.concatenate([rows * m for m in masks], axis=1)
            block = ref[0, g * GROUP : (g + 1) * GROUP].reshape(GROUP * width, width)
            parts.append(dot(left, block, (1, 0)))
        return jnp.concatenate(parts, axis=0)

    def backward(ref, vectors):
        parts = []
        for g in range(count // GROUP):
            rows = vectors[g * GROUP : (g + 1) * GROUP]
            block = ref[0, g * GROUP : (g + 1) * GROUP].reshape(GROUP * width, width)
            every = dot(rows, block, (1, 1))
            total = jnp.zeros((GROUP, width), F32)
            for k in range(GROUP):
                total = jnp.where(line == k, every[:, k * width : (k + 1) * width], total)
            parts.append(total)
        return jnp.concatenate(parts, axis=0)

    def wait_all(buffer, number, sem):
        piece = buffer.at[pl.ds(0, number)]
        pltpu.make_async_copy(piece, piece, sem).wait()

    def send_cut(turn, w, stats):
        wb = jnp.broadcast_to(w, (GROUP, width)).astype(BF)
        products = forward(cuts, lambda g: wb)
        placed = spread(slot_table, products, (1, 0)).reshape(owners, STRIDE, width)
        if stats is None:
            stats = placed - placed.astype(BF).astype(F32)
        send_a[turn] = jnp.concatenate([placed, stats], axis=1).astype(BF)
        recv_a[turn, flat] = send_a[turn, c]
        if turn == 0:
            pl.semaphore_wait(barrier, n_dev - 1)

        def go(k, carry):
            other = lax.rem(flat + k, n_dev)
            oc, orow = lax.rem(other, owners), other // owners
            pltpu.make_async_remote_copy(
                src_ref=send_a.at[turn, oc],
                dst_ref=recv_a.at[turn, flat],
                send_sem=sem_a.at[0, turn],
                recv_sem=sem_a.at[1, turn],
                device_id={"col": oc, "row": orow},
                device_id_type=MESH,
            ).start()
            return carry

        lax.fori_loop(1, n_dev, go, 0)

    def send_rows(turn, y, moved):
        yg = dot(row_table, y.astype(BF), (0, 0)).astype(BF)
        products = forward(tiles, lambda g: yg[g * GROUP : (g + 1) * GROUP])
        send_r[turn, :blocks] = spread(col_table, products, (1, 0))
        send_r[turn, blocks:] = moved
        recv_r[turn, r] = send_r[turn]

        def go(k, carry):
            pltpu.make_async_remote_copy(
                src_ref=send_r.at[turn],
                dst_ref=recv_r.at[turn, r],
                send_sem=sem_r.at[0, turn],
                recv_sem=sem_r.at[1, turn],
                device_id={"col": c, "row": lax.rem(r + k, n_row)},
                device_id_type=MESH,
            ).start()
            return carry

        lax.fori_loop(1, n_row, go, 0)

    def to_columns(source, dest_ref, sems, turn):
        def go(k, carry):
            oc = lax.rem(c + k, owners)
            pltpu.make_async_remote_copy(
                src_ref=source(oc),
                dst_ref=dest_ref.at[turn, c],
                send_sem=sems.at[0, turn],
                recv_sem=sems.at[1, turn],
                device_id={"col": oc, "row": r},
                device_id_type=MESH,
            ).start()
            return carry

        lax.fori_loop(1, owners, go, 0)

    w = w0[...]
    send_cut(0, w, chosen.reshape(owners, STRIDE, width))
    for load in loads[4:]:
        load.wait()
    row_table = one_hot(row_of[...], row_blocks).astype(BF)
    col_table = one_hot(col_of[...], blocks).astype(BF)
    x, y = x0[...], y0[...]
    send_rows(0, y, jnp.zeros((STRIDE, width), F32))

    eta = jnp.full((1, 1), step[0], F32)
    omega = jnp.full((1, 1), weight[0], F32)
    held = None
    for turn in range(ITERS + 1):
        wait_all(recv_a.at[turn], n_dev - 1, sem_a.at[1, turn])
        landed = recv_a[turn].astype(F32)
        prices = landed[:, :STRIDE].reshape(n_dev * STRIDE, width).astype(BF)
        beside = landed[:, STRIDE:]
        if turn == 0:
            held = beside.reshape(n_dev * STRIDE, width).astype(BF)
        cut_part = dot(held, prices, (0, 0))
        if turn == ITERS:
            low = beside.reshape(n_dev * STRIDE, width).astype(BF)
            cut_part = cut_part + dot(held, low, (0, 0))
        cut_part = cut_part[:blocks]
        wait_all(recv_r.at[turn], n_row - 1, sem_r.at[1, turn])
        from_rows = recv_r[turn, 0]
        for other in range(1, n_row):
            from_rows = from_rows + recv_r[turn, other]
        grad = cost[...] + (cut_part - from_rows[:blocks])
        if turn == 1:
            stats = jnp.sum(beside, axis=0)
            moved = jnp.sum(stats[0:1] + stats[1:2] + stats[2:3], axis=1, keepdims=True)
            dual_moved = jnp.sum(
                (stats[3:4] + stats[4:5] + stats[5:6])
                + jnp.sum(from_rows[blocks:], axis=0, keepdims=True),
                axis=1,
                keepdims=True,
            )
            omega = jnp.sqrt(omega * jnp.sqrt((moved + EPSILON) / (dual_moved + EPSILON)))
        if turn == ITERS:
            break
        tau = eta / omega
        sigma = eta * omega
        new_x = jnp.clip(x - tau * grad, 0.0, 1.0)
        xbar = (2.0 * new_x - x).astype(BF)

        mine = (
            recv_a[0, pl.ds(r * owners, owners)]
            .astype(F32)[:, STRIDE:]
            .reshape(slots, width)[:, :blocks]
            .astype(BF)
        )
        send_x[turn] = dot(mine, xbar, (1, 0)).reshape(owners, STRIDE, width)
        recv_x[turn, c] = send_x[turn, c]
        to_columns(lambda oc: send_x.at[turn, oc], recv_x, sem_x, turn)

        xg = dot(col_table, xbar, (0, 0)).astype(BF)
        send_p[turn] = spread(row_table, backward(tiles, xg), (1, 0)).astype(BF)
        recv_p[turn, c] = send_p[turn]
        to_columns(lambda oc: send_p.at[turn], recv_p, sem_p, turn)

        wait_all(recv_x.at[turn], owners - 1, sem_x.at[1, turn])
        xr = recv_x[turn].reshape(slots, width).astype(BF)
        xk = dot(slot_table, xr, (0, 0)).astype(BF)
        activity = jnp.sum(backward(cuts, xk), axis=0, keepdims=True)
        new_w = jnp.maximum(w + sigma * (activity - 1.0), 0.0)
        place = lax.broadcasted_iota(jnp.int32, (STRIDE, width), 0)
        step_x = jnp.where(r == 0, 1.0, 0.0) * (new_x - x)
        step_w = new_w - w
        stats = None
        if turn + 1 < ITERS:
            pieces = split3(jnp.sum(step_x * step_x, axis=0, keepdims=True)) + split3(step_w * step_w)
            stats = jnp.zeros((STRIDE, width), F32)
            for at, piece in enumerate(pieces):
                stats = jnp.where(place == at, piece.astype(F32), stats)
            stats = jnp.broadcast_to(stats[None], (owners, STRIDE, width))
        send_cut(turn + 1, new_w, stats)

        wait_all(recv_p.at[turn], owners - 1, sem_p.at[1, turn])
        total = jnp.sum(recv_p[turn].astype(F32), axis=0)
        new_y = jnp.maximum(y + sigma * (demand[...] - total), 0.0)
        step_y = new_y - y
        squares = jnp.sum((step_y * step_y).reshape(row_blocks // STRIDE, STRIDE, width), axis=0)
        send_rows(turn + 1, new_y, squares)
        x, y, w = new_x, new_y, new_w

    x_out[...] = x
    y_out[...] = y
    w_out[...] = w
    here = lax.broadcasted_iota(jnp.int32, (blocks, blocks), 0) == lax.broadcasted_iota(
        jnp.int32, (blocks, blocks), 1
    )
    power = jnp.exp2(exps[...].astype(F32))
    limit = -0.125 * jnp.sum(jnp.where(here, power, 0.0), axis=1, keepdims=True)
    v_out[...] = jnp.maximum(limit - grad, 0.0)

    for turn in range(ITERS + 1):
        wait_all(recv_a.at[turn], n_dev - 1, sem_a.at[0, turn])
        wait_all(recv_r.at[turn], n_row - 1, sem_r.at[0, turn])
        if turn < ITERS:
            wait_all(recv_x.at[turn], owners - 1, sem_x.at[0, turn])
            wait_all(recv_p.at[turn], owners - 1, sem_p.at[0, turn])


def hand_out(*refs):
    sem = refs[8]
    copies = [pltpu.make_async_copy(refs[i], refs[4 + i], sem.at[i]) for i in range(4)]
    for copy in copies:
        copy.start()
    for copy in copies:
        copy.wait()


def local(
    covering_tiles,
    tile_row_blocks,
    tile_cols,
    cut_tiles,
    cut_dest,
    cut_cols,
    cost,
    demand,
    primal_start,
    initial_duals,
    cut_start,
    primal_weight,
    step_size,
    exponents,
    owners,
    n_row,
):
    blocks, width = cost.shape
    row_blocks = demand.shape[0]
    n_dev = owners * n_row
    phases = ITERS + 1
    vmem = pl.BlockSpec(memory_space=pltpu.VMEM)
    smem = pl.BlockSpec(memory_space=pltpu.SMEM)
    operands = (
        cut_dest.reshape(cut_cols.shape),
        cut_cols,
        cut_start,
        cut_tiles,
        tile_row_blocks,
        initial_duals,
        covering_tiles,
        tile_cols,
        primal_start,
        cost,
        demand,
        exponents.reshape(1, blocks),
    )
    results = pl.pallas_call(
        functools.partial(kernel, owners, n_row),
        out_shape=(
            jax.ShapeDtypeStruct(primal_start.shape, F32),
            jax.ShapeDtypeStruct(initial_duals.shape, F32),
            jax.ShapeDtypeStruct(cut_start.shape, F32),
            jax.ShapeDtypeStruct(cost.shape, F32),
        ),
        in_specs=[pl.BlockSpec(memory_space=pltpu.HBM)] * 12 + [smem] * 2,
        out_specs=(vmem,) * 4,
        scratch_shapes=[
            pltpu.VMEM((phases, owners, 2 * STRIDE, width), BF),
            pltpu.VMEM((phases, n_dev, 2 * STRIDE, width), BF),
            pltpu.VMEM((ITERS, owners, STRIDE, width), F32),
            pltpu.VMEM((ITERS, owners, STRIDE, width), F32),
            pltpu.VMEM((ITERS, row_blocks, width), BF),
            pltpu.VMEM((ITERS, owners, row_blocks, width), BF),
            pltpu.VMEM((phases, blocks + STRIDE, width), F32),
            pltpu.VMEM((phases, n_row, blocks + STRIDE, width), F32),
            *[pltpu.VMEM(a.shape, a.dtype) for a in operands],
            pltpu.SemaphoreType.DMA((len(operands),)),
            pltpu.SemaphoreType.DMA((2, phases)),
            pltpu.SemaphoreType.DMA((2, ITERS)),
            pltpu.SemaphoreType.DMA((2, ITERS)),
            pltpu.SemaphoreType.DMA((2, phases)),
        ],
        compiler_params=pltpu.CompilerParams(
            collective_id=0, has_side_effects=True, vmem_limit_bytes=64 * 1024 * 1024
        ),
        name="pdhg",
    )(*operands, primal_weight, step_size)
    anywhere = pl.BlockSpec(memory_space=pl.ANY)
    return pl.pallas_call(
        hand_out,
        out_shape=tuple(jax.ShapeDtypeStruct(a.shape, a.dtype) for a in results),
        in_specs=[anywhere] * 4,
        out_specs=(anywhere,) * 4,
        scratch_shapes=[pltpu.SemaphoreType.DMA((4,))],
        compiler_params=pltpu.CompilerParams(vmem_limit_bytes=64 * 1024 * 1024),
        name="hand_out",
    )(*results)


def solution(mesh):
    in_specs = (
        P("row", "col", None, None),
        P("row", "col"),
        P("row", "col"),
        P("col", "row", None, None),
        P("col", "row", None),
        P("col", "row"),
        P("col", None),
        P("row", None),
        P("col", None),
        P("row", None),
        P("col", "row"),
        P(),
        P(),
        P("col"),
    )
    out_specs = (P("col", None), P("row", None), P("col", "row"), P("col", None))
    body = functools.partial(local, owners=mesh.shape["col"], n_row=mesh.shape["row"])
    return jax.shard_map(body, mesh=mesh, in_specs=in_specs, out_specs=out_specs, check_vma=False)
```

```python
import functools

import jax
import jax.numpy as jnp
from jax import lax
from jax.experimental import pallas as pl
from jax.experimental.pallas import tpu as pltpu
from jax.sharding import PartitionSpec as P

ITERS = 2
EPSILON = 1e-06
GROUP = 16
STRIDE = 8
BF = jnp.bfloat16
F32 = jnp.float32
MESH = pl.DeviceIdType.MESH


def dot(a, b, contract):
    return lax.dot_general(a, b, ((contract[:1], contract[1:]), ((), ())), preferred_element_type=F32)


def split3(values):
    high = values.astype(BF)
    rest = values - high.astype(F32)
    middle = rest.astype(BF)
    low = (rest - middle.astype(F32)).astype(BF)
    return high, middle, low


def spread(table, values, contract):
    high, middle, low = split3(values)
    return dot(table, high, contract) + (dot(table, middle, contract) + dot(table, low, contract))


def kernel(
    owners,
    n_row,
    far_dest,
    far_cut_col,
    far_w0,
    far_cuts,
    far_row_of,
    far_y0,
    far_tiles,
    far_col_of,
    far_x0,
    far_cost,
    far_demand,
    far_exps,
    weight,
    step,
    x_out,
    y_out,
    w_out,
    v_out,
    send_a,
    recv_a,
    send_x,
    recv_x,
    send_p,
    recv_p,
    send_r,
    recv_r,
    dest,
    cut_col,
    w0,
    cuts,
    row_of,
    y0,
    tiles,
    col_of,
    x0,
    cost,
    demand,
    exps,
    sem_in,
    sem_a,
    sem_x,
    sem_p,
    sem_r,
):
    far = (far_dest, far_cut_col, far_w0, far_cuts, far_row_of, far_y0)
    far += (far_tiles, far_col_of, far_x0, far_cost, far_demand, far_exps)
    near = (dest, cut_col, w0, cuts, row_of, y0, tiles, col_of, x0, cost, demand, exps)
    loads = [pltpu.make_async_copy(a, b, sem_in.at[i]) for i, (a, b) in enumerate(zip(far, near))]
    for load in loads:
        load.start()
    c = lax.axis_index("col")
    r = lax.axis_index("row")
    n_dev = owners * n_row
    flat = r * owners + c
    count = tiles.shape[1]
    blocks, width = cost.shape
    row_blocks = demand.shape[0]
    slots = owners * STRIDE

    barrier = pltpu.get_barrier_semaphore()

    def greet(k, carry):
        other = lax.rem(flat + k, n_dev)
        pl.semaphore_signal(
            barrier,
            inc=1,
            device_id={"col": lax.rem(other, owners), "row": other // owners},
            device_id_type=MESH,
        )
        return carry

    lax.fori_loop(1, n_dev, greet, 0)

    for load in loads[:4]:
        load.wait()

    def one_hot(row, size):
        return jnp.where(
            lax.broadcasted_iota(jnp.int32, (size, row.shape[1]), 0) == row, 1.0, 0.0
        )

    owner_table = one_hot(dest[...], max(owners, 16)).astype(BF)
    same = dot(owner_table, owner_table, (0, 0))
    earlier = lax.broadcasted_iota(jnp.int32, same.shape, 0) < lax.broadcasted_iota(
        jnp.int32, same.shape, 1
    )
    rank = jnp.sum(jnp.where(earlier, same, 0.0), axis=0, keepdims=True).astype(jnp.int32)
    slot_table = one_hot(dest[...] * STRIDE + rank, slots).astype(BF)
    block_table = one_hot(cut_col[...], width).astype(BF)
    chosen = dot(slot_table, block_table, (1, 1))

    line = lax.broadcasted_iota(jnp.int32, (GROUP, width), 0)
    masks = [jnp.where(line == k, 1.0, 0.0).astype(BF) for k in range(GROUP)]

    def forward(ref, rows_at):
        parts = []
        for g in range(count // GROUP):
            rows = rows_at(g)
            left = jnp.concatenate([rows * m for m in masks], axis=1)
            block = ref[0, g * GROUP : (g + 1) * GROUP].reshape(GROUP * width, width)
            parts.append(dot(left, block, (1, 0)))
        return jnp.concatenate(parts, axis=0)

    def backward(ref, vectors):
        parts = []
        for g in range(count // GROUP):
            rows = vectors[g * GROUP : (g + 1) * GROUP]
            block = ref[0, g * GROUP : (g + 1) * GROUP].reshape(GROUP * width, width)
            every = dot(rows, block, (1, 1))
            total = jnp.zeros((GROUP, width), F32)
            for k in range(GROUP):
                total = jnp.where(line == k, every[:, k * width : (k + 1) * width], total)
            parts.append(total)
        return jnp.concatenate(parts, axis=0)

    def wait_all(buffer, number, sem):
        piece = buffer.at[pl.ds(0, number)]
        pltpu.make_async_copy(piece, piece, sem).wait()

    def send_cut(turn, w, stats):
        wb = jnp.broadcast_to(w, (GROUP, width)).astype(BF)
        products = forward(cuts, lambda g: wb)
        placed = spread(slot_table, products, (1, 0)).reshape(owners, STRIDE, width)
        if stats is None:
            stats = placed - placed.astype(BF).astype(F32)
        send_a[turn] = jnp.concatenate([placed, stats], axis=1).astype(BF)
        recv_a[turn, flat] = send_a[turn, c]
        if turn == 0:
            pl.semaphore_wait(barrier, n_dev - 1)

        def go(k, carry):
            other = lax.rem(flat + k, n_dev)
            oc, orow = lax.rem(other, owners), other // owners
            pltpu.make_async_remote_copy(
                src_ref=send_a.at[turn, oc],
                dst_ref=recv_a.at[turn, flat],
                send_sem=sem_a.at[0, turn],
                recv_sem=sem_a.at[1, turn],
                device_id={"col": oc, "row": orow},
                device_id_type=MESH,
            ).start()
            return carry

        lax.fori_loop(1, n_dev, go, 0)

    def send_rows(turn, y, moved):
        yg = dot(row_table, y.astype(BF), (0, 0)).astype(BF)
        products = forward(tiles, lambda g: yg[g * GROUP : (g + 1) * GROUP])
        send_r[turn, :blocks] = spread(col_table, products, (1, 0))
        send_r[turn, blocks:] = moved
        recv_r[turn, r] = send_r[turn]

        def go(k, carry):
            pltpu.make_async_remote_copy(
                src_ref=send_r.at[turn],
                dst_ref=recv_r.at[turn, r],
                send_sem=sem_r.at[0, turn],
                recv_sem=sem_r.at[1, turn],
                device_id={"col": c, "row": lax.rem(r + k, n_row)},
                device_id_type=MESH,
            ).start()
            return carry

        lax.fori_loop(1, n_row, go, 0)

    def to_columns(source, dest_ref, sems, turn):
        def go(k, carry):
            oc = lax.rem(c + k, owners)
            pltpu.make_async_remote_copy(
                src_ref=source(oc),
                dst_ref=dest_ref.at[turn, c],
                send_sem=sems.at[0, turn],
                recv_sem=sems.at[1, turn],
                device_id={"col": oc, "row": r},
                device_id_type=MESH,
            ).start()
            return carry

        lax.fori_loop(1, owners, go, 0)

    w = w0[...]
    send_cut(0, w, chosen.reshape(owners, STRIDE, width))
    for load in loads[4:]:
        load.wait()
    row_table = one_hot(row_of[...], row_blocks).astype(BF)
    col_table = one_hot(col_of[...], blocks).astype(BF)
    x, y = x0[...], y0[...]
    send_rows(0, y, jnp.zeros((STRIDE, width), F32))

    eta = jnp.full((1, 1), step[0], F32)
    omega = jnp.full((1, 1), weight[0], F32)
    held = None
    for turn in range(ITERS + 1):
        wait_all(recv_a.at[turn], n_dev - 1, sem_a.at[1, turn])
        landed = recv_a[turn].astype(F32)
        prices = landed[:, :STRIDE].reshape(n_dev * STRIDE, width).astype(BF)
        beside = landed[:, STRIDE:]
        if turn == 0:
            held = beside.reshape(n_dev * STRIDE, width).astype(BF)
        cut_part = dot(held, prices, (0, 0))
        if turn == ITERS:
            low = beside.reshape(n_dev * STRIDE, width).astype(BF)
            cut_part = cut_part + dot(held, low, (0, 0))
        cut_part = cut_part[:blocks]
        wait_all(recv_r.at[turn], n_row - 1, sem_r.at[1, turn])
        from_rows = recv_r[turn, 0]
        for other in range(1, n_row):
            from_rows = from_rows + recv_r[turn, other]
        grad = cost[...] + (cut_part - from_rows[:blocks])
        if turn == 1:
            stats = jnp.sum(beside, axis=0)
            moved = jnp.sum(stats[0:1] + stats[1:2] + stats[2:3], axis=1, keepdims=True)
            dual_moved = jnp.sum(
                (stats[3:4] + stats[4:5] + stats[5:6])
                + jnp.sum(from_rows[blocks:], axis=0, keepdims=True),
                axis=1,
                keepdims=True,
            )
            omega = jnp.sqrt(omega * jnp.sqrt((moved + EPSILON) / (dual_moved + EPSILON)))
        if turn == ITERS:
            break
        tau = eta / omega
        sigma = eta * omega
        new_x = jnp.clip(x - tau * grad, 0.0, 1.0)
        xbar = (2.0 * new_x - x).astype(BF)

        mine = (
            recv_a[0, pl.ds(r * owners, owners)]
            .astype(F32)[:, STRIDE:]
            .reshape(slots, width)[:, :blocks]
            .astype(BF)
        )
        send_x[turn] = dot(mine, xbar, (1, 0)).reshape(owners, STRIDE, width)
        recv_x[turn, c] = send_x[turn, c]
        to_columns(lambda oc: send_x.at[turn, oc], recv_x, sem_x, turn)

        xg = dot(col_table, xbar, (0, 0)).astype(BF)
        send_p[turn] = spread(row_table, backward(tiles, xg), (1, 0)).astype(BF)
        recv_p[turn, c] = send_p[turn]
        to_columns(lambda oc: send_p.at[turn], recv_p, sem_p, turn)

        wait_all(recv_x.at[turn], owners - 1, sem_x.at[1, turn])
        xr = recv_x[turn].reshape(slots, width).astype(BF)
        xk = dot(slot_table, xr, (0, 0)).astype(BF)
        activity = jnp.sum(backward(cuts, xk), axis=0, keepdims=True)
        new_w = jnp.maximum(w + sigma * (activity - 1.0), 0.0)
        place = lax.broadcasted_iota(jnp.int32, (STRIDE, width), 0)
        step_x = jnp.where(r == 0, 1.0, 0.0) * (new_x - x)
        step_w = new_w - w
        stats = None
        if turn + 1 < ITERS:
            pieces = split3(jnp.sum(step_x * step_x, axis=0, keepdims=True)) + split3(step_w * step_w)
            stats = jnp.zeros((STRIDE, width), F32)
            for at, piece in enumerate(pieces):
                stats = jnp.where(place == at, piece.astype(F32), stats)
            stats = jnp.broadcast_to(stats[None], (owners, STRIDE, width))
        send_cut(turn + 1, new_w, stats)

        wait_all(recv_p.at[turn], owners - 1, sem_p.at[1, turn])
        total = jnp.sum(recv_p[turn].astype(F32), axis=0)
        new_y = jnp.maximum(y + sigma * (demand[...] - total), 0.0)
        step_y = new_y - y
        squares = jnp.sum((step_y * step_y).reshape(row_blocks // STRIDE, STRIDE, width), axis=0)
        send_rows(turn + 1, new_y, squares)
        x, y, w = new_x, new_y, new_w

    x_out[...] = x
    y_out[...] = y
    w_out[...] = w
    here = lax.broadcasted_iota(jnp.int32, (blocks, blocks), 0) == lax.broadcasted_iota(
        jnp.int32, (blocks, blocks), 1
    )
    power = jnp.exp2(exps[...].astype(F32))
    limit = -0.125 * jnp.sum(jnp.where(here, power, 0.0), axis=1, keepdims=True)
    v_out[...] = jnp.maximum(limit - grad, 0.0)

    for turn in range(ITERS + 1):
        wait_all(recv_a.at[turn], n_dev - 1, sem_a.at[0, turn])
        wait_all(recv_r.at[turn], n_row - 1, sem_r.at[0, turn])
        if turn < ITERS:
            wait_all(recv_x.at[turn], owners - 1, sem_x.at[0, turn])
            wait_all(recv_p.at[turn], owners - 1, sem_p.at[0, turn])


def hand_out(*refs):
    for source, target in zip(refs[:4], refs[4:]):
        target[...] = source[...]


def local(
    covering_tiles,
    tile_row_blocks,
    tile_cols,
    cut_tiles,
    cut_dest,
    cut_cols,
    cost,
    demand,
    primal_start,
    initial_duals,
    cut_start,
    primal_weight,
    step_size,
    exponents,
    owners,
    n_row,
):
    blocks, width = cost.shape
    row_blocks = demand.shape[0]
    n_dev = owners * n_row
    phases = ITERS + 1
    vmem = pl.BlockSpec(memory_space=pltpu.VMEM)
    smem = pl.BlockSpec(memory_space=pltpu.SMEM)
    operands = (
        cut_dest.reshape(cut_cols.shape),
        cut_cols,
        cut_start,
        cut_tiles,
        tile_row_blocks,
        initial_duals,
        covering_tiles,
        tile_cols,
        primal_start,
        cost,
        demand,
        exponents.reshape(1, blocks),
    )
    results = pl.pallas_call(
        functools.partial(kernel, owners, n_row),
        out_shape=(
            jax.ShapeDtypeStruct(primal_start.shape, F32),
            jax.ShapeDtypeStruct(initial_duals.shape, F32),
            jax.ShapeDtypeStruct(cut_start.shape, F32),
            jax.ShapeDtypeStruct(cost.shape, F32),
        ),
        in_specs=[pl.BlockSpec(memory_space=pltpu.HBM)] * 12 + [smem] * 2,
        out_specs=(vmem,) * 4,
        scratch_shapes=[
            pltpu.VMEM((phases, owners, 2 * STRIDE, width), BF),
            pltpu.VMEM((phases, n_dev, 2 * STRIDE, width), BF),
            pltpu.VMEM((ITERS, owners, STRIDE, width), F32),
            pltpu.VMEM((ITERS, owners, STRIDE, width), F32),
            pltpu.VMEM((ITERS, row_blocks, width), BF),
            pltpu.VMEM((ITERS, owners, row_blocks, width), BF),
            pltpu.VMEM((phases, blocks + STRIDE, width), F32),
            pltpu.VMEM((phases, n_row, blocks + STRIDE, width), F32),
            *[pltpu.VMEM(a.shape, a.dtype) for a in operands],
            pltpu.SemaphoreType.DMA((len(operands),)),
            pltpu.SemaphoreType.DMA((2, phases)),
            pltpu.SemaphoreType.DMA((2, ITERS)),
            pltpu.SemaphoreType.DMA((2, ITERS)),
            pltpu.SemaphoreType.DMA((2, phases)),
        ],
        compiler_params=pltpu.CompilerParams(
            collective_id=0, has_side_effects=True, vmem_limit_bytes=64 * 1024 * 1024
        ),
        name="pdhg",
    )(*operands, primal_weight, step_size)
    return pl.pallas_call(
        hand_out,
        out_shape=tuple(jax.ShapeDtypeStruct(a.shape, a.dtype) for a in results),
        in_specs=[vmem] * 4,
        out_specs=(vmem,) * 4,
        compiler_params=pltpu.CompilerParams(vmem_limit_bytes=64 * 1024 * 1024),
        name="hand_out",
    )(*results)


def solution(mesh):
    in_specs = (
        P("row", "col", None, None),
        P("row", "col"),
        P("row", "col"),
        P("col", "row", None, None),
        P("col", "row", None),
        P("col", "row"),
        P("col", None),
        P("row", None),
        P("col", None),
        P("row", None),
        P("col", "row"),
        P(),
        P(),
        P("col"),
    )
    out_specs = (P("col", None), P("row", None), P("col", "row"), P("col", None))
    body = functools.partial(local, owners=mesh.shape["col"], n_row=mesh.shape["row"])
    return jax.shard_map(body, mesh=mesh, in_specs=in_specs, out_specs=out_specs, check_vma=False)
```
